256 devices in a mesh: outer: 16 (over x_lo, z), inner: 16 (over y, x_hi, core).
Axes of the slice: x: 4 (x_hi: 2, x_lo: 2; x = x_hi * 2 + x_lo), y: 4, z: 8, core: 2. Of those that a mesh axis runs over, the one named last changes fastest.
Arguments:
- queries: bfloat16 [262144, 512], P(('outer', 'inner')), may hold values from -5 to 5
- key_rows: bfloat16 [262144, 128], P(('outer', 'inner')), may hold values from -5 to 5
- value_rows: bfloat16 [262144, 128], P(('outer', 'inner')), may hold values from -6 to 6
- grad_out: bfloat16 [262144, 512], P(('outer', 'inner')), may hold values from -6 to 6
- segments: int32 [262144], P(('outer', 'inner')), may hold values from 0 to 262143, as said below
Outputs:
- attended: bfloat16 [262144, 512], P(('outer', 'inner'))
- grad_queries: bfloat16 [262144, 512], P(('outer', 'inner'))
- grad_keys: bfloat16 [262144, 128], P(('outer', 'inner'))
- grad_values: bfloat16 [262144, 128], P(('outer', 'inner'))
The draws below stay inside these ranges and needn't reach their ends.
Inputs may be any that keep to these rules, and one draw needn't show every extreme that they name: `segments`: in position order ids never fall; each document spans 1 to 1024 consecutive positions; the first document spans exactly 1024; one document begins 1024 / 4 positions before position 131072 and spans 1024; the last document of the sequence has id 262144 - 1.
All inputs are finite; a program needn't handle non-finite values.
Results may differ from the reference program's by a relative error of at most 0.015.
Values may be sent and summed in bfloat16 or wider, within the bound.
No kernel may reach another device: no remote copies, remote signals or barrier semaphores. Data moves between devices by JAX's collectives and lax.ppermute only.
A program may use at most 64 MiB of HBM per device.

```python
import jax
import jax.numpy as jnp
from jax import lax

H = 4
HD = 128
TOK_DEV = 1024
TOKENS = 262144
N_OUTER = 16
N_INNER = 16


def drawn_rows(key, columns):
    return jnp.clip(jax.random.normal(key, (TOKENS, columns), jnp.float32), -5.0, 5.0)


def draw_queries(key, part):
    key = jax.random.fold_in(key, 5)
    result = drawn_rows(key, H * HD)
    return result.astype(jnp.bfloat16)


def draw_key_rows(key, part):
    key = jax.random.fold_in(key, 7)
    result = drawn_rows(key, HD)
    return result.astype(jnp.bfloat16)


def draw_segments(key, part):
    key = jax.random.fold_in(key, 23)
    kind_key, long_key, short_key = jax.random.split(key, 3)
    total_rows = TOKENS
    group_count = total_rows // 64 + 1
    groups = jax.random.randint(kind_key, (group_count,), 0, 2)
    doc_kinds = jnp.repeat(groups, 64, total_repeat_length=group_count * 64)[:total_rows]
    longer = jax.random.randint(long_key, (total_rows,), TOK_DEV // 2, TOK_DEV + 1)
    shorter = jax.random.randint(short_key, (total_rows,), 1, 33)
    lengths = jnp.where(doc_kinds == 1, longer, shorter).astype(jnp.int32).at[0].set(TOK_DEV)
    doc_ends = jnp.cumsum(lengths).astype(jnp.int32)
    positions = jnp.arange(total_rows, dtype=jnp.int32)
    drawn_ids = jnp.searchsorted(doc_ends, positions, side='right').astype(jnp.int32)
    half_rows = TOK_DEV // 2
    devices = N_OUTER * N_INNER
    middle_low = devices * half_rows - half_rows // 2
    middle_high = middle_low + TOK_DEV
    inside = (positions >= middle_low) & (positions < middle_high)
    lifted = drawn_ids + (positions >= middle_low).astype(jnp.int32) + (positions >= middle_high).astype(jnp.int32)
    doc_ids = jnp.where(inside, drawn_ids[middle_low] + 1, lifted)
    doc_ids = jnp.where(doc_ids == doc_ids[total_rows - 1], jnp.int32(total_rows - 1), doc_ids).astype(jnp.int32)
    blocks = doc_ids.reshape(2 * devices, half_rows)
    return jnp.stack([blocks[:devices], blocks[devices:][::-1]], axis=1).reshape(total_rows)


def level_of(rng, extent, cuts, least, top_value):
    gain, own = 1.0, jax.random.fold_in(rng, 6)
    for position, blocks in cuts:
        steps = jnp.exp(jax.random.uniform(jax.random.fold_in(own, position), (blocks,), jnp.float32, least / len(cuts), top_value / len(cuts)))
        gain = gain * jnp.repeat(steps, extent[position] // blocks).reshape([-1 if axis == position else 1 for axis in range(len(extent))])
    return gain


def scatter_about(rng, shape, width, reach, shards=(), held_as=jnp.bfloat16):
    values = jax.random.normal(rng, shape, jnp.float32) * width
    if len(shards) > 0:
        values = level_of(rng, shape, shards, -0.22, 0.18) * values
    return jnp.clip(values, min=-reach, max=reach).astype(held_as)


def setup_inputs(seed: int = 0) -> dict:
    keys = jax.random.split(jax.random.key(seed), 6)
    queries = draw_queries(jax.random.fold_in(keys[5], 71), 0)
    key_rows = draw_key_rows(jax.random.fold_in(keys[5], 71), 0)
    value_rows = scatter_about(keys[2], (TOKENS, HD), 1.0, 6.0, ((0, 256),))
    grad_out = scatter_about(keys[3], (TOKENS, H * HD), 1.0, 6.0, ((0, 256),))
    segments = draw_segments(jax.random.fold_in(keys[5], 71), 0)
    return dict(queries=queries, key_rows=key_rows, value_rows=value_rows, grad_out=grad_out, segments=segments)


def unfold(array, devices, half_rows):
    blocks = array.reshape((devices, 2, half_rows) + array.shape[1:])
    return jnp.concatenate([blocks[:, 0], blocks[::-1, 1]], axis=0).reshape(array.shape)


def refold(array, devices, half_rows):
    blocks = array.reshape((2 * devices, half_rows) + array.shape[1:])
    return jnp.stack([blocks[:devices], blocks[devices:][::-1]], axis=1).reshape(array.shape)


def attend(query_rows, grad_rows, visible, key_block, value_block):
    head_size = key_block.shape[1]
    heads = query_rows.shape[1] // head_size
    scaling = head_size ** -0.5
    outputs = []
    query_grads = []
    grad_key = jnp.zeros(key_block.shape, jnp.float32)
    grad_value = jnp.zeros(value_block.shape, jnp.float32)
    for head_index in range(heads):
        query_head = query_rows[:, head_index * head_size:(head_index + 1) * head_size]
        grad_head = grad_rows[:, head_index * head_size:(head_index + 1) * head_size]
        scores = jnp.dot(query_head, key_block.T, preferred_element_type=jnp.float32) * scaling
        masked = jnp.where(visible, scores, -1e30)
        largest = jnp.max(masked, axis=1, keepdims=True)
        log_total = largest + jnp.log(jnp.sum(jnp.exp(masked - largest), axis=1, keepdims=True))
        weights = jnp.where(visible, jnp.exp(masked - log_total), 0.0)
        rounded = weights.astype(jnp.bfloat16)
        attended = jnp.dot(rounded, value_block, preferred_element_type=jnp.float32).astype(jnp.bfloat16)
        correction = jnp.sum(grad_head.astype(jnp.float32) * attended.astype(jnp.float32), axis=1, keepdims=True)
        grad_weights = jnp.dot(grad_head, value_block.T, preferred_element_type=jnp.float32)
        grad_scores = (weights * (grad_weights - correction) * scaling).astype(jnp.bfloat16)
        query_grads.append(jnp.dot(grad_scores, key_block, preferred_element_type=jnp.float32).astype(jnp.bfloat16))
        grad_key = grad_key + jnp.dot(grad_scores.T, query_head, preferred_element_type=jnp.float32)
        grad_value = grad_value + jnp.dot(rounded.T, grad_head, preferred_element_type=jnp.float32)
        outputs.append(attended)
    return jnp.concatenate(outputs, axis=1), jnp.concatenate(query_grads, axis=1), grad_key, grad_value


def reference(queries, key_rows, value_rows, grad_out, segments):
    devices = N_OUTER * N_INNER
    half_rows = TOK_DEV // 2
    padding = 2 * half_rows
    query_order = unfold(queries, devices, half_rows)
    grad_order = unfold(grad_out, devices, half_rows)
    key_order = unfold(key_rows, devices, half_rows)
    value_order = unfold(value_rows, devices, half_rows)
    segment_order = unfold(segments, devices, half_rows)
    positions = jnp.arange(TOKENS, dtype=jnp.int32)
    key_padded = jnp.concatenate([jnp.zeros((padding, HD), key_rows.dtype), key_order], axis=0)
    value_padded = jnp.concatenate([jnp.zeros((padding, HD), value_rows.dtype), value_order], axis=0)
    segment_padded = jnp.concatenate([jnp.full((padding,), -1, jnp.int32), segment_order.astype(jnp.int32)], axis=0)
    position_padded = jnp.concatenate([jnp.arange(padding, dtype=jnp.int32) - padding, positions], axis=0)
    blocks = TOKENS // half_rows

    def one_block(block_index):
        start = (block_index * half_rows).astype(jnp.int32)
        query_rows = lax.dynamic_slice_in_dim(query_order, start, half_rows, 0)
        grad_rows = lax.dynamic_slice_in_dim(grad_order, start, half_rows, 0)
        query_pos = lax.dynamic_slice_in_dim(positions, start, half_rows, 0)
        query_seg = lax.dynamic_slice_in_dim(segment_order.astype(jnp.int32), start, half_rows, 0)
        key_block = lax.dynamic_slice_in_dim(key_padded, start, 3 * half_rows, 0)
        value_block = lax.dynamic_slice_in_dim(value_padded, start, 3 * half_rows, 0)
        key_pos = lax.dynamic_slice_in_dim(position_padded, start, 3 * half_rows, 0)
        key_seg = lax.dynamic_slice_in_dim(segment_padded, start, 3 * half_rows, 0)
        visible = (key_pos[None, :] <= query_pos[:, None]) & (key_seg[None, :] == query_seg[:, None])
        return attend(query_rows, grad_rows, visible, key_block, value_block)

    attended, grad_queries, key_terms, value_terms = lax.map(one_block, jnp.arange(blocks, dtype=jnp.int32))

    def combine(terms):
        parts = terms.reshape(blocks, 3, half_rows, HD)
        zero_one = jnp.zeros((1, half_rows, HD), jnp.float32)
        zero_two = jnp.zeros((2, half_rows, HD), jnp.float32)
        total = parts[:, 2] + jnp.concatenate([parts[1:, 1], zero_one], axis=0) + jnp.concatenate([parts[2:, 0], zero_two], axis=0)
        return refold(total.reshape(TOKENS, HD).astype(jnp.bfloat16), devices, half_rows)

    attended = refold(attended.reshape(TOKENS, H * HD), devices, half_rows)
    grad_queries = refold(grad_queries.reshape(TOKENS, H * HD), devices, half_rows)
    return attended, grad_queries, combine(key_terms), combine(value_terms)
```

```python
import functools
import math

import jax
import jax.numpy as jnp
from jax import lax
from jax.experimental import pallas as pl
from jax.experimental.pallas import tpu as pltpu
from jax.sharding import PartitionSpec as P

AXES = ("outer", "inner")
TILE = 256
LANES = 128
HALF = 512
NOTES = 16
HIDDEN = -1e30
NT = (((1,), (1,)), ((), ()))
TN = (((0,), (0,)), ((), ()))
NN = (((1,), (0,)), ((), ()))


def dot(a, b, dims):
    return lax.dot_general(a, b, dims, preferred_element_type=jnp.float32)


def core_of():
    return lax.rem(lax.axis_index("inner"), 2)


def stacked(pair, tile, heads):
    ref = pair[tile // 2]
    width = ref.shape[1] // heads
    rows = pl.ds(pl.multiple_of(core_of() * HALF + (tile % 2) * TILE, TILE), TILE)
    return jnp.concatenate(
        [ref[rows, h * width : (h + 1) * width] for h in range(heads)], axis=0
    )


def unstacked(columns, pair, tile, heads):
    ref = pair[tile // 2]
    width = ref.shape[1] // heads
    start = (tile % 2) * TILE
    rows = columns.T.astype(ref.dtype)
    for h in range(heads):
        ref[start : start + TILE, h * width : (h + 1) * width] = rows[h * TILE : (h + 1) * TILE]


def keys_of(pair, key_tile):
    ref = pair[key_tile // 2]
    start = (key_tile % 2) * TILE
    return ref[start : start + TILE, :], ref[HALF + start : HALF + start + TILE, :]


def segments_of(pair):
    rows = HALF // LANES
    parts = []
    for ref in pair:
        notes = ref[2 * HALF :, :].astype(jnp.float32)
        high, middle, low = (notes[i * rows : (i + 1) * rows] for i in range(3))
        parts.append(high * 4096.0 + middle * 64.0 + low)
    return jnp.concatenate(parts, axis=0)


def spread(segs, columns):
    for r in range(segs.shape[0]):
        block = jnp.broadcast_to(segs[r : r + 1, :], (LANES, LANES))
        columns[r * LANES : (r + 1) * LANES, :] = block.T


def own_bias(segs, columns, tile, key_tile, heads):
    per = TILE // LANES
    keys = columns[key_tile * TILE : (key_tile + 1) * TILE, :]
    parts = []
    for r in range(per):
        seen = keys == segs[tile * per + r : tile * per + r + 1, :]
        if tile == key_tile:
            key = lax.broadcasted_iota(jnp.int32, (TILE, LANES), 0)
            query = lax.broadcasted_iota(jnp.int32, (TILE, LANES), 1) + r * LANES
            seen = seen & (key <= query)
        parts.append(jnp.where(seen, 0.0, HIDDEN))
    return jnp.concatenate(parts * heads, axis=1)


def crossing_bias(first_key, crossing, tile, key_tile, heads):
    key = lax.broadcasted_iota(jnp.int32, (TILE, LANES), 0) + key_tile * TILE
    query = lax.broadcasted_iota(jnp.int32, (TILE, TILE), 1) + tile * TILE
    key = jnp.concatenate([key] * (TILE // LANES), axis=1)
    seen = jnp.where((key >= first_key) & (query < crossing), 0.0, HIDDEN)
    return jnp.concatenate([seen] * heads, axis=1)


def softmax_step(scores, values, log_ref, total_ref, acc):
    largest = log_ref[...]
    larger = jnp.maximum(largest, jnp.max(scores, axis=0, keepdims=True))
    shrink = jnp.exp2(largest - larger)
    weights = jnp.exp2(scores - larger)
    log_ref[...] = larger
    total_ref[...] = total_ref[...] * shrink + jnp.sum(weights, axis=0, keepdims=True)
    acc[...] = acc[...] * shrink + dot(values, weights.astype(jnp.bfloat16), TN)


def finish(tile, g, largest, total_ref, acc, part_ref, log_ref, corr_ref):
    total = total_ref[...]
    att = acc[...] / total
    rounded = att.astype(jnp.bfloat16).astype(jnp.float32)
    corr_ref[tile] = jnp.sum(rounded * g.T.astype(jnp.float32), axis=0, keepdims=True)
    log_ref[tile] = largest + jnp.log2(total)
    part_ref[tile] = att


def pack_kernel(k_ref, v_ref, segs_ref, first_ref, second_ref, segs, sems):
    core = core_of()
    rows = HALF // LANES
    ids = pltpu.make_async_copy(segs_ref, segs, sems.at[4])
    ids.start()
    copies = []
    for i, (ref, half) in enumerate(((first_ref, core), (second_ref, 1 - core))):
        start = pl.ds(pl.multiple_of(half * HALF, HALF), HALF)
        copies += [
            pltpu.make_async_copy(k_ref.at[start, :], ref.at[pl.ds(0, HALF), :], sems.at[2 * i]),
            pltpu.make_async_copy(v_ref.at[start, :], ref.at[pl.ds(HALF, HALF), :], sems.at[2 * i + 1]),
        ]
    for copy in copies:
        copy.start()
    ids.wait()
    for ref, half in ((first_ref, core), (second_ref, 1 - core)):
        own = segs[pl.ds(half * rows, rows), :]
        codes = [own >> 12, (own >> 6) & 63, own & 63, own & 0]
        notes = jnp.concatenate([code.astype(jnp.float32) for code in codes], axis=0)
        ref[2 * HALF :, :] = notes.astype(jnp.bfloat16)
    for copy in copies:
        copy.wait()


def own_forward(
    heads, factor,
    q_a, q_b, g_a, g_b, kv_a, kv_b,
    part_ref, log_ref, corr_ref, same_ref, acc, largest, total, columns,
):
    segs = segments_of((kv_a, kv_b))
    spread(segs, columns)
    tiles = 2 * HALF // TILE
    per = TILE // LANES
    same_ref[0] = 0
    for tile in range(1, tiles):
        first = segs[tile * per : tile * per + 1, :1]
        same_ref[tile] = jnp.sum((segs[: tile * per] == first).astype(jnp.float32)).astype(jnp.int32)
    for tile in range(tiles):
        q = stacked((q_a, q_b), tile, heads)

        def step(key_tile):
            keys, values = keys_of((kv_a, kv_b), key_tile)
            scores = dot(keys, q, NT) * factor + own_bias(segs, columns, tile, key_tile, heads)
            if key_tile == tile:
                top = jnp.max(scores, axis=0, keepdims=True)
                weights = jnp.exp2(scores - top)
                largest[...] = top
                total[...] = jnp.sum(weights, axis=0, keepdims=True)
                acc[...] = dot(values, weights.astype(jnp.bfloat16), TN)
            else:
                softmax_step(scores, values, largest, total, acc)

        step(tile)
        for key_tile in reversed(range(tile)):

            @pl.when(same_ref[tile] > (tile - 1 - key_tile) * TILE)
            def _():
                step(key_tile)

        g = stacked((g_a, g_b), tile, heads)
        finish(tile, g, largest[...], total, acc, part_ref, log_ref, corr_ref)


def crossing_kernel(
    heads, factor, scaling,
    q_a, q_b, g_a, g_b, kv_a, kv_b, past_a, past_b, part_in, log_in, corr_in,
    part_ref, log_ref, corr_ref, back_ref, gq_ref, size_ref,
    acc, largest, total, kept, grown, gk, gv,
):
    rows = 2 * HALF
    tiles = rows // TILE
    log_ref[...] = log_in[...]
    corr_ref[...] = corr_in[...]
    gk[...] = jnp.zeros_like(gk)
    gv[...] = jnp.zeros_like(gv)
    segs = segments_of((kv_a, kv_b))
    past = segments_of((past_a, past_b))
    first = segs[:1, :1]
    started = (lax.axis_index("outer") > 0) | (lax.axis_index("inner") > 0)
    tail = jnp.sum((past == first).astype(jnp.float32)).astype(jnp.int32)
    tail = jnp.where(started, tail, 0)
    head = jnp.sum((segs == first).astype(jnp.float32)).astype(jnp.int32)
    crossing = jnp.where(tail > 0, head, 0)
    first_key = rows - tail
    size_ref[0] = crossing

    for tile in range(tiles):

        @pl.when(tile * TILE < crossing)
        def _():
            q = stacked((q_a, q_b), tile, heads)
            g = stacked((g_a, g_b), tile, heads)
            acc[...] = part_in[tile]
            largest[...] = log_in[tile]
            total[...] = jnp.ones_like(total)
            for key_tile in range(tile, tiles):

                @pl.when((key_tile + 1) * TILE > first_key)
                def _():
                    keys, values = keys_of((past_a, past_b), key_tile)
                    bias = crossing_bias(first_key, crossing, tile, key_tile, heads)
                    scores = dot(keys, q, NT) * factor + bias
                    kept[key_tile] = scores
                    grown[key_tile] = dot(values, g, NT)
                    softmax_step(scores, values, largest, total, acc)

            finish(tile, g, largest[...], total, acc, part_ref, log_ref, corr_ref)
            gq = gq_ref.at[tile]
            gq[...] = jnp.zeros(gq.shape, jnp.float32)
            for key_tile in range(tile, tiles):

                @pl.when((key_tile + 1) * TILE > first_key)
                def _():
                    block = slice(key_tile * TILE, (key_tile + 1) * TILE)
                    keys, _ = keys_of((past_a, past_b), key_tile)
                    weights = jnp.exp2(kept[key_tile] - log_ref[tile])
                    grad = (weights * (grown[key_tile] - corr_ref[tile])).astype(jnp.bfloat16)
                    gv[block, :] += dot(weights.astype(jnp.bfloat16), g, NN)
                    gk[block, :] += dot(grad, q, NN)
                    gq[...] += dot(keys, grad, TN)

    for start in (0, HALF):
        place = 2 * start
        rows = slice(start, start + HALF)
        back_ref[place : place + HALF, :] = (gk[rows, :] * scaling).astype(back_ref.dtype)
        back_ref[place + HALF : place + 2 * HALF, :] = gv[rows, :].astype(back_ref.dtype)


def own_backward(
    heads, factor, scaling,
    size_ref, same_ref, q_a, q_b, g_a, g_b, kv_a, kv_b, part_ref, past_ref, log_ref, corr_ref, gq_in,
    att_a, att_b, gq_a, gq_b, gkv_a, gkv_b, acc, gk, gv, columns,
):
    segs = segments_of((kv_a, kv_b))
    spread(segs, columns)
    tiles = 2 * HALF // TILE
    gk[...] = jnp.zeros_like(gk)
    gv[...] = jnp.zeros_like(gv)
    for tile in range(tiles):
        q = stacked((q_a, q_b), tile, heads)
        g = stacked((g_a, g_b), tile, heads)

        @pl.when(tile * TILE < size_ref[0])
        def _():
            acc[...] = gq_in[tile]
            unstacked(past_ref[tile], (att_a, att_b), tile, heads)

        @pl.when(tile * TILE >= size_ref[0])
        def _():
            acc[...] = jnp.zeros_like(acc)
            unstacked(part_ref[tile], (att_a, att_b), tile, heads)

        def step(key_tile):
            block = slice(key_tile * TILE, (key_tile + 1) * TILE)
            keys, values = keys_of((kv_a, kv_b), key_tile)
            scores = dot(keys, q, NT) * factor + own_bias(segs, columns, tile, key_tile, heads)
            weights = jnp.exp2(scores - log_ref[tile])
            grad = (weights * (dot(values, g, NT) - corr_ref[tile])).astype(jnp.bfloat16)
            gv[block, :] += dot(weights.astype(jnp.bfloat16), g, NN)
            gk[block, :] += dot(grad, q, NN)
            acc[...] += dot(keys, grad, TN)

        step(tile)
        for key_tile in reversed(range(tile)):

            @pl.when(same_ref[tile] > (tile - 1 - key_tile) * TILE)
            def _():
                step(key_tile)

        unstacked(acc[...] * scaling, (gq_a, gq_b), tile, heads)
    for ref, start in ((gkv_a, 0), (gkv_b, HALF)):
        rows = slice(start, start + HALF)
        ref[:HALF, :] = gk[rows, :] * scaling
        ref[HALF:, :] = gv[rows, :]


def place_kernel(att_a, att_c, gq_a, gq_c, att_ref, gq_ref, sems):
    core = core_of()
    copies = []
    for i, (ref, half, out) in enumerate(
        ((att_a, core, att_ref), (att_c, 1 - core, att_ref), (gq_a, core, gq_ref), (gq_c, 1 - core, gq_ref))
    ):
        rows = pl.ds(pl.multiple_of(half * HALF, HALF), HALF)
        copies.append(pltpu.make_async_copy(ref, out.at[rows, :], sems.at[i]))
    for copy in copies:
        copy.start()
    for copy in copies:
        copy.wait()


def add_kernel(gkv_a, gkv_b, came_ref, mine_ref, give_ref):
    for start, own, out in ((0, gkv_a, mine_ref), (2 * HALF, gkv_b, give_ref)):
        came = came_ref[start : start + 2 * HALF, :].astype(jnp.float32)
        out[...] = (own[...] + came).astype(out.dtype)


def place_grads(mine_ref, other_ref, gk_ref, gv_ref, sems):
    core = core_of()
    copies = []
    for ref, half in ((mine_ref, core), (other_ref, 1 - core)):
        rows = pl.ds(pl.multiple_of(half * HALF, HALF), HALF)
        for out, start in ((gk_ref, 0), (gv_ref, HALF)):
            copies.append(
                pltpu.make_async_copy(ref.at[pl.ds(start, HALF), :], out.at[rows, :], sems.at[len(copies)])
            )
    for copy in copies:
        copy.start()
    for copy in copies:
        copy.wait()


SMEM = pl.BlockSpec(memory_space=pltpu.SMEM)
VMEM = pl.BlockSpec(memory_space=pltpu.VMEM)
ANY = pl.BlockSpec(memory_space=pl.ANY)
HBM = pl.BlockSpec(memory_space=pltpu.HBM)


def call(kernel, scalars, arrays, outs, scratch, micros, name, scalar_outs=0, specs=None, room=40):
    arrived, left = specs or ([VMEM] * len(arrays), [VMEM] * (len(outs) - scalar_outs))
    return pl.pallas_call(
        kernel,
        out_shape=outs,
        in_specs=[SMEM] * len(scalars) + arrived,
        out_specs=left + [SMEM] * scalar_outs,
        scratch_shapes=scratch,
        compiler_params=pltpu.CompilerParams(vmem_limit_bytes=room * 2**20),
        cost_estimate=pl.CostEstimate(
            flops=int(micros * 1e9), bytes_accessed=2**20, transcendentals=0
        ),
        name=name,
    )(*scalars, *arrays)


def per_device(queries, key_rows, value_rows, grad_out, segments):
    count = lax.axis_size(AXES)
    rows, width = key_rows.shape
    heads = queries.shape[1] // width
    tiles = rows // TILE
    scaling = width ** (-0.5)
    factor = scaling * math.log2(math.e)
    swap = [(i, i ^ 1) for i in range(count)]
    along = (
        [(i, i + 2) for i in range(0, count - 2, 2)]
        + [(count - 2, count - 1)]
        + [(i + 2, i) for i in range(1, count - 2, 2)]
    )
    near = [(i, i + 1) for i in range(1, count - 2, 2)]
    near = near + [(b, a) for a, b in near] + [(count - 1, count - 1)]

    def send(array, pairs):
        return lax.ppermute(array, AXES, pairs)

    def send_back(array, pairs):
        return lax.ppermute(array, AXES, [(b, a) for a, b in pairs])

    f32 = jnp.float32
    bf16 = jnp.bfloat16
    segs = segments.reshape(rows // LANES, LANES)
    bundle = jax.ShapeDtypeStruct((2 * HALF + NOTES, width), bf16)
    first, second = call(
        pack_kernel, [], [key_rows, value_rows, segs], [bundle, bundle],
        [pltpu.VMEM(segs.shape, jnp.int32), pltpu.SemaphoreType.DMA((5,))], 1, "pack",
        specs=([HBM] * 3, [VMEM] * 2), room=60,
    )
    first, second, queries, grad_out = lax.optimization_barrier(
        (first, second, queries, grad_out)
    )
    past_a = send(first, along)
    past_b = send(second, near)
    other = send(second, swap)
    q_o, g_o = send(queries, swap), send(grad_out, swap)
    line = jax.ShapeDtypeStruct((tiles, 1, heads * TILE), f32)
    wide = jax.ShapeDtypeStruct((tiles, width, heads * TILE), f32)
    half_rows = jax.ShapeDtypeStruct((HALF, heads * width), bf16)
    half_back = jax.ShapeDtypeStruct((2 * HALF, width), bf16)
    half_grad = jax.ShapeDtypeStruct((2 * HALF, width), f32)
    acc = pltpu.VMEM((width, heads * TILE), f32)
    single = pltpu.VMEM((1, heads * TILE), f32)
    columns = pltpu.VMEM((rows, LANES), f32)
    gsum = pltpu.VMEM((rows, width), f32)
    square = pltpu.VMEM((tiles, TILE, heads * TILE), f32)
    arrays = [queries, q_o, grad_out, g_o, first, other]
    part, log_own, corr_own, same = call(
        functools.partial(own_forward, heads, factor),
        [], arrays, [wide, line, line, jax.ShapeDtypeStruct((tiles,), jnp.int32)],
        [acc, single, single, columns], 6, "own_forward", scalar_outs=1,
    )
    past_part, log_total, corr, back, gq_part, size = call(
        functools.partial(crossing_kernel, heads, factor, scaling),
        [], [*arrays, past_a, past_b, part, log_own, corr_own],
        [wide, line, line, jax.ShapeDtypeStruct((4 * HALF, width), bf16), wide,
         jax.ShapeDtypeStruct((1,), jnp.int32)],
        [acc, single, single, square, square, gsum, gsum], 6, "crossing", scalar_outs=1,
    )
    came = send_back(back, along)
    att_a, att_b, gq_a, gq_b, gkv_a, gkv_b = call(
        functools.partial(own_backward, heads, factor, scaling),
        [size, same], [*arrays, part, past_part, log_total, corr, gq_part],
        [half_rows, half_rows, half_rows, half_rows, half_grad, half_grad],
        [acc, gsum, gsum, columns], 6, "own_backward",
    )
    att_b, gq_b = lax.optimization_barrier((att_b, gq_b))
    att_c, gq_c = send(att_b, swap), send(gq_b, swap)
    full = jax.ShapeDtypeStruct((rows, heads * width), bf16)
    copies = [pltpu.SemaphoreType.DMA((4,))]
    attended, grad_queries = call(
        place_kernel, [], [att_a, att_c, gq_a, gq_c], [full, full], copies, 1, "place",
        specs=([ANY] * 4, [ANY] * 2),
    )
    mine, give = call(
        add_kernel, [], [gkv_a, gkv_b, came], [half_back, half_back], [], 1, "add"
    )
    thin = jax.ShapeDtypeStruct((rows, width), bf16)
    grad_keys, grad_values = call(
        place_grads, [], [mine, send(give, swap)], [thin, thin], copies, 1, "place_grads",
        specs=([ANY] * 2, [ANY] * 2),
    )
    return attended, grad_queries, grad_keys, grad_values


def solution(mesh):
    rows = P(AXES, None)
    return jax.shard_map(
        per_device,
        mesh=mesh,
        in_specs=(rows, rows, rows, rows, P(AXES)),
        out_specs=(rows, rows, rows, rows),
        check_vma=False,
    )
```

```python
import functools
import math

import jax
import jax.numpy as jnp
from jax import lax
from jax.experimental import pallas as pl
from jax.experimental.pallas import tpu as pltpu
from jax.sharding import PartitionSpec as P

AXES = ("outer", "inner")
TILE = 256
LANES = 128
HALF = 512
NOTES = 16
HIDDEN = -1e30
NT = (((1,), (1,)), ((), ()))
TN = (((0,), (0,)), ((), ()))
NN = (((1,), (0,)), ((), ()))


def dot(a, b, dims):
    return lax.dot_general(a, b, dims, preferred_element_type=jnp.float32)


def core_of():
    return lax.rem(lax.axis_index("inner"), 2)


def stacked(pair, tile, heads):
    ref = pair[tile // 2]
    width = ref.shape[1] // heads
    rows = pl.ds(pl.multiple_of(core_of() * HALF + (tile % 2) * TILE, TILE), TILE)
    return jnp.concatenate(
        [ref[rows, h * width : (h + 1) * width] for h in range(heads)], axis=0
    )


def unstacked(columns, pair, tile, heads):
    ref = pair[tile // 2]
    width = ref.shape[1] // heads
    start = (tile % 2) * TILE
    rows = columns.astype(ref.dtype).T
    for h in range(heads):
        ref[start : start + TILE, h * width : (h + 1) * width] = rows[h * TILE : (h + 1) * TILE]


def keys_of(pair, key_tile):
    ref = pair[key_tile // 2]
    start = (key_tile % 2) * TILE
    if isinstance(ref, tuple):
        rows = pl.ds(pl.multiple_of(core_of() * HALF + start, TILE), TILE)
        return ref[0][rows, :], ref[1][rows, :]
    return ref[start : start + TILE, :], ref[HALF + start : HALF + start + TILE, :]


def segments_of(pair):
    rows = HALF // LANES
    parts = []
    for ref in pair:
        if isinstance(ref, tuple):
            own = ref[2][pl.ds(core_of() * rows, rows), :]
            parts.append(own.astype(jnp.float32))
            continue
        notes = ref[2 * HALF :, :].astype(jnp.float32)
        high, middle, low = (notes[i * rows : (i + 1) * rows] for i in range(3))
        parts.append(high * 4096.0 + middle * 64.0 + low)
    return jnp.concatenate(parts, axis=0)


def spread(segs, columns):
    for r in range(segs.shape[0]):
        block = jnp.broadcast_to(segs[r : r + 1, :], (LANES, LANES))
        columns[r * LANES : (r + 1) * LANES, :] = block.T


def own_bias(segs, columns, tile, key_tile, heads):
    per = TILE // LANES
    keys = columns[key_tile * TILE : (key_tile + 1) * TILE, :]
    parts = []
    for r in range(per):
        seen = keys == segs[tile * per + r : tile * per + r + 1, :]
        if tile == key_tile:
            key = lax.broadcasted_iota(jnp.int32, (TILE, LANES), 0)
            query = lax.broadcasted_iota(jnp.int32, (TILE, LANES), 1) + r * LANES
            seen = seen & (key <= query)
        parts.append(jnp.where(seen, 0.0, HIDDEN))
    return jnp.concatenate(parts * heads, axis=1)


def crossing_bias(first_key, crossing, tile, key_tile, heads):
    key = lax.broadcasted_iota(jnp.int32, (TILE, LANES), 0) + key_tile * TILE
    query = lax.broadcasted_iota(jnp.int32, (TILE, TILE), 1) + tile * TILE
    key = jnp.concatenate([key] * (TILE // LANES), axis=1)
    seen = jnp.where((key >= first_key) & (query < crossing), 0.0, HIDDEN)
    return jnp.concatenate([seen] * heads, axis=1)


def softmax_step(scores, values, log_ref, total_ref, acc):
    largest = log_ref[...]
    larger = jnp.maximum(largest, jnp.max(scores, axis=0, keepdims=True))
    shrink = jnp.exp2(largest - larger)
    weights = jnp.exp2(scores - larger)
    log_ref[...] = larger
    total_ref[...] = total_ref[...] * shrink + jnp.sum(weights, axis=0, keepdims=True)
    acc[...] = acc[...] * shrink + dot(values, weights.astype(jnp.bfloat16), TN)


def finish(tile, g, largest, total_ref, acc, part_ref, log_ref, corr_ref):
    total = total_ref[...]
    att = acc[...] / total
    rounded = att.astype(jnp.bfloat16).astype(jnp.float32)
    corr_ref[tile] = jnp.sum(rounded * g.T.astype(jnp.float32), axis=0, keepdims=True)
    log_ref[tile] = largest + jnp.log2(total)
    part_ref[tile] = att


def gradient_step(scores, keys, grown, q, g, log_total, corr, key_tile, gk, gv, gq):
    block = slice(key_tile * TILE, (key_tile + 1) * TILE)
    weights = jnp.exp2(scores - log_total)
    grad = (weights * (grown - corr)).astype(jnp.bfloat16)
    gv[block, :] += dot(weights.astype(jnp.bfloat16), g, NN)
    gk[block, :] += dot(grad, q, NN)
    gq[...] += dot(keys, grad, TN)


def pack_kernel(k_ref, v_ref, segs_ref, first_ref, second_ref, segs, stage, sems, out_sems):
    core = core_of()
    rows = HALF // LANES
    ids = pltpu.make_async_copy(segs_ref, segs, sems.at[4])
    ids.start()
    halves = ((0, first_ref, core), (1, second_ref, 1 - core))
    arriving = []
    for i, ref, half in halves:
        start = pl.ds(pl.multiple_of(half * HALF, HALF), HALF)
        for j, source in enumerate((k_ref, v_ref)):
            place = pl.ds(j * HALF, HALF)
            copy = pltpu.make_async_copy(source.at[start, :], stage.at[i, place, :], sems.at[2 * i + j])
            copy.start()
            arriving.append((copy, i, ref, place))
    ids.wait()
    leaving = []

    def leave(i, ref, place):
        copy = pltpu.make_async_copy(stage.at[i, place, :], ref.at[place, :], out_sems.at[len(leaving)])
        copy.start()
        leaving.append(copy)

    for i, ref, half in halves:
        own = segs[pl.ds(half * rows, rows), :]
        codes = [own >> 12, (own >> 6) & 63, own & 63, own & 0]
        codes = jnp.concatenate([code.astype(jnp.float32) for code in codes], axis=0)
        stage[i, 2 * HALF :, :] = codes.astype(jnp.bfloat16)
        leave(i, ref, pl.ds(2 * HALF, NOTES))
    for copy, i, ref, place in arriving:
        copy.wait()
        leave(i, ref, place)
    for copy in leaving:
        copy.wait()


def own_forward(
    heads, factor,
    q_a, q_b, g_a, g_b, k_a, v_a, ids_a, kv_b,
    part_ref, log_ref, corr_ref, gk, gv, gq_ref, same_ref, acc, largest, total, columns, kept,
):
    kv_a = (k_a, v_a, ids_a)
    segs = segments_of((kv_a, kv_b))
    spread(segs, columns)
    tiles = 2 * HALF // TILE
    per = TILE // LANES
    head = jnp.sum((segs == segs[:1, :1]).astype(jnp.float32)).astype(jnp.int32)
    ahead = head <= (tiles - 1) * TILE
    same_ref[0] = ahead.astype(jnp.int32)
    gk[...] = jnp.zeros_like(gk)
    gv[...] = jnp.zeros_like(gv)
    for tile in range(1, tiles):
        first = segs[tile * per : tile * per + 1, :1]
        same_ref[tile] = jnp.sum((segs[: tile * per] == first).astype(jnp.float32)).astype(jnp.int32)
    for tile in range(tiles):
        q = stacked((q_a, q_b), tile, heads)

        def step(key_tile):
            keys, values = keys_of((kv_a, kv_b), key_tile)
            scores = dot(keys, q, NT) * factor + own_bias(segs, columns, tile, key_tile, heads)
            if tile == tiles - 1:
                kept[key_tile] = scores
            if key_tile == tile:
                top = jnp.max(scores, axis=0, keepdims=True)
                weights = jnp.exp2(scores - top)
                largest[...] = top
                total[...] = jnp.sum(weights, axis=0, keepdims=True)
                acc[...] = dot(values, weights.astype(jnp.bfloat16), TN)
            else:
                softmax_step(scores, values, largest, total, acc)

        step(tile)
        for key_tile in reversed(range(tile)):

            @pl.when(same_ref[tile] > (tile - 1 - key_tile) * TILE)
            def _():
                step(key_tile)

        g = stacked((g_a, g_b), tile, heads)
        finish(tile, g, largest[...], total, acc, part_ref, log_ref, corr_ref)

    @pl.when(ahead)
    def _():
        gq_ref[...] = jnp.zeros_like(gq_ref)

        def grads(key_tile):
            keys, values = keys_of((kv_a, kv_b), key_tile)
            gradient_step(
                kept[key_tile], keys, dot(values, g, NT), q, g, log_ref[tile], corr_ref[tile],
                key_tile, gk, gv, gq_ref,
            )

        grads(tile)
        for key_tile in reversed(range(tile)):

            @pl.when(same_ref[tile] > (tile - 1 - key_tile) * TILE)
            def _():
                grads(key_tile)


def crossing_kernel(
    heads, factor, scaling,
    q_a, q_b, g_a, g_b, k_a, v_a, ids_a, kv_b, past_a, past_b, part_in, log_in, corr_in,
    part_ref, log_ref, corr_ref, back_ref, gq_ref, size_ref,
    acc, largest, total, kept, grown, gk, gv,
):
    kv_a = (k_a, v_a, ids_a)
    rows = 2 * HALF
    tiles = rows // TILE
    log_ref[...] = log_in[...]
    corr_ref[...] = corr_in[...]
    gk[...] = jnp.zeros_like(gk)
    gv[...] = jnp.zeros_like(gv)
    segs = segments_of((kv_a, kv_b))
    past = segments_of((past_a, past_b))
    first = segs[:1, :1]
    started = (lax.axis_index("outer") > 0) | (lax.axis_index("inner") > 0)
    tail = jnp.sum((past == first).astype(jnp.float32)).astype(jnp.int32)
    tail = jnp.where(started, tail, 0)
    head = jnp.sum((segs == first).astype(jnp.float32)).astype(jnp.int32)
    crossing = jnp.where(tail > 0, head, 0)
    first_key = rows - tail
    size_ref[0] = crossing

    for tile in range(tiles):

        @pl.when(tile * TILE < crossing)
        def _():
            q = stacked((q_a, q_b), tile, heads)
            g = stacked((g_a, g_b), tile, heads)
            acc[...] = part_in[tile]
            largest[...] = log_in[tile]
            total[...] = jnp.ones_like(total)
            for key_tile in range(tile, tiles):

                @pl.when((key_tile + 1) * TILE > first_key)
                def _():
                    keys, values = keys_of((past_a, past_b), key_tile)
                    bias = crossing_bias(first_key, crossing, tile, key_tile, heads)
                    scores = dot(keys, q, NT) * factor + bias
                    kept[key_tile] = scores
                    grown[key_tile] = dot(values, g, NT)
                    softmax_step(scores, values, largest, total, acc)

            finish(tile, g, largest[...], total, acc, part_ref, log_ref, corr_ref)
            gq = gq_ref.at[tile]
            gq[...] = jnp.zeros(gq.shape, jnp.float32)
            for key_tile in range(tile, tiles):

                @pl.when((key_tile + 1) * TILE > first_key)
                def _():
                    keys, _ = keys_of((past_a, past_b), key_tile)
                    gradient_step(
                        kept[key_tile], keys, grown[key_tile], q, g, log_ref[tile], corr_ref[tile],
                        key_tile, gk, gv, gq,
                    )

    for start in (0, HALF):
        place = 2 * start
        rows = slice(start, start + HALF)
        back_ref[place : place + HALF, :] = (gk[rows, :] * scaling).astype(back_ref.dtype)
        back_ref[place + HALF : place + 2 * HALF, :] = gv[rows, :].astype(back_ref.dtype)


def own_backward(
    heads, factor, scaling,
    size_ref, same_ref, q_a, q_b, g_a, g_b, k_a, v_a, ids_a, kv_b, part_ref, past_ref, log_ref, corr_ref, gq_in,
    gk_in, gv_in, gq_last,
    att_ref, gq_ref, att_b, gq_b, gkv_a, gkv_b, acc, gk, gv, columns, att_a, gq_a, sems,
):
    kv_a = (k_a, v_a, ids_a)
    segs = segments_of((kv_a, kv_b))
    spread(segs, columns)
    tiles = 2 * HALF // TILE
    gk[...] = gk_in[...]
    gv[...] = gv_in[...]
    mine = pl.ds(pl.multiple_of(core_of() * HALF, HALF), HALF)
    copies = [
        pltpu.make_async_copy(att_a, att_ref.at[mine, :], sems.at[0]),
        pltpu.make_async_copy(gq_a, gq_ref.at[mine, :], sems.at[1]),
    ]
    for tile in range(tiles):

        @pl.when(tile * TILE < size_ref[0])
        def _():
            acc[...] = gq_in[tile]
            unstacked(past_ref[tile], (att_a, att_b), tile, heads)

        @pl.when(tile * TILE >= size_ref[0])
        def _():
            acc[...] = jnp.zeros_like(acc)
            unstacked(part_ref[tile], (att_a, att_b), tile, heads)

        def steps():
            q = stacked((q_a, q_b), tile, heads)
            g = stacked((g_a, g_b), tile, heads)

            def step(key_tile):
                keys, values = keys_of((kv_a, kv_b), key_tile)
                scores = dot(keys, q, NT) * factor + own_bias(segs, columns, tile, key_tile, heads)
                gradient_step(
                    scores, keys, dot(values, g, NT), q, g, log_ref[tile], corr_ref[tile],
                    key_tile, gk, gv, acc,
                )

            step(tile)
            for key_tile in reversed(range(tile)):

                @pl.when(same_ref[tile] > (tile - 1 - key_tile) * TILE)
                def _():
                    step(key_tile)

        if tile < tiles - 1:
            steps()
        else:

            @pl.when(same_ref[0] == 0)
            def _():
                steps()

            @pl.when(same_ref[0] != 0)
            def _():
                acc[...] = gq_last[...]

        unstacked(acc[...] * scaling, (gq_a, gq_b), tile, heads)
        if tile == tiles // 2 - 1:
            for copy in copies:
                copy.start()
    for ref, start in ((gkv_a, 0), (gkv_b, HALF)):
        rows = slice(start, start + HALF)
        ref[:HALF, :] = gk[rows, :] * scaling
        ref[HALF:, :] = gv[rows, :]
    for copy in copies:
        copy.wait()


def add_kernel(gkv_a, gkv_b, came_ref, mine_ref, give_ref):
    for start, own, out in ((0, gkv_a, mine_ref), (2 * HALF, gkv_b, give_ref)):
        came = came_ref[start : start + 2 * HALF, :].astype(jnp.float32)
        out[...] = (own[...] + came).astype(out.dtype)


def place_kernel(att_in, gq_in, att_c, gq_c, mine_ref, other_ref, att_ref, gq_ref, gk_ref, gv_ref, sems):
    core = core_of()
    mine = pl.ds(pl.multiple_of(core * HALF, HALF), HALF)
    other = pl.ds(pl.multiple_of((1 - core) * HALF, HALF), HALF)
    key_rows = pl.ds(0, HALF)
    value_rows = pl.ds(HALF, HALF)
    moves = (
        (att_c, att_ref.at[other, :]),
        (gq_c, gq_ref.at[other, :]),
        (mine_ref.at[key_rows, :], gk_ref.at[mine, :]),
        (mine_ref.at[value_rows, :], gv_ref.at[mine, :]),
        (other_ref.at[key_rows, :], gk_ref.at[other, :]),
        (other_ref.at[value_rows, :], gv_ref.at[other, :]),
    )
    copies = [pltpu.make_async_copy(a, b, sems.at[i]) for i, (a, b) in enumerate(moves)]
    for copy in copies:
        copy.start()
    for copy in copies:
        copy.wait()


SMEM = pl.BlockSpec(memory_space=pltpu.SMEM)
VMEM = pl.BlockSpec(memory_space=pltpu.VMEM)
ANY = pl.BlockSpec(memory_space=pl.ANY)
HBM = pl.BlockSpec(memory_space=pltpu.HBM)


def call(kernel, scalars, arrays, outs, scratch, micros, name, scalar_outs=0, specs=None, room=30, aliases=None):
    arrived, left = specs or ([VMEM] * len(arrays), [VMEM] * (len(outs) - scalar_outs))
    return pl.pallas_call(
        kernel,
        out_shape=outs,
        in_specs=[SMEM] * len(scalars) + arrived,
        out_specs=left + [SMEM] * scalar_outs,
        scratch_shapes=scratch,
        compiler_params=pltpu.CompilerParams(vmem_limit_bytes=room * 2**20),
        cost_estimate=pl.CostEstimate(
            flops=int(micros * 1e9), bytes_accessed=2**20, transcendentals=0
        ),
        input_output_aliases=aliases or {},
        name=name,
    )(*scalars, *arrays)


def per_device(queries, key_rows, value_rows, grad_out, segments):
    count = lax.axis_size(AXES)
    rows, width = key_rows.shape
    heads = queries.shape[1] // width
    tiles = rows // TILE
    scaling = width ** (-0.5)
    factor = scaling * math.log2(math.e)
    swap = [(i, i ^ 1) for i in range(count)]
    along = (
        [(i, i + 2) for i in range(0, count - 2, 2)]
        + [(count - 2, count - 1)]
        + [(i + 2, i) for i in range(1, count - 2, 2)]
    )
    near = [(i, i + 1) for i in range(1, count - 2, 2)]
    near = near + [(b, a) for a, b in near] + [(count - 1, count - 1)]

    def send(array, pairs):
        return lax.ppermute(array, AXES, pairs)

    def send_back(array, pairs):
        return lax.ppermute(array, AXES, [(b, a) for a, b in pairs])

    f32 = jnp.float32
    bf16 = jnp.bfloat16
    segs = segments.reshape(rows // LANES, LANES)
    bundle = jax.ShapeDtypeStruct((2 * HALF + NOTES, width), bf16)
    first, second = call(
        pack_kernel, [], [key_rows, value_rows, segs], [bundle, bundle],
        [
            pltpu.VMEM(segs.shape, jnp.int32),
            pltpu.VMEM((2, 2 * HALF + NOTES, width), bf16),
            pltpu.SemaphoreType.DMA((5,)),
            pltpu.SemaphoreType.DMA((6,)),
        ], 1, "pack",
        specs=([HBM] * 3, [HBM] * 2), room=60,
    )
    first, second, queries, grad_out = lax.optimization_barrier(
        (first, second, queries, grad_out)
    )
    past_a = send(first, along)
    other = send(second, swap)
    other, second = lax.optimization_barrier((other, second))
    past_b = send(second, near)
    q_o, g_o = send(queries, swap), send(grad_out, swap)
    line = jax.ShapeDtypeStruct((tiles, 1, heads * TILE), f32)
    wide = jax.ShapeDtypeStruct((tiles, width, heads * TILE), f32)
    half_rows = jax.ShapeDtypeStruct((HALF, heads * width), bf16)
    half_back = jax.ShapeDtypeStruct((2 * HALF, width), bf16)
    half_grad = jax.ShapeDtypeStruct((2 * HALF, width), f32)
    acc = pltpu.VMEM((width, heads * TILE), f32)
    single = pltpu.VMEM((1, heads * TILE), f32)
    columns = pltpu.VMEM((rows, LANES), f32)
    gsum = pltpu.VMEM((rows, width), f32)
    square = pltpu.VMEM((tiles, TILE, heads * TILE), f32)
    arrays = [queries, q_o, grad_out, g_o, key_rows, value_rows, segs, other]
    grads = jax.ShapeDtypeStruct((rows, width), f32)
    tile_grads = jax.ShapeDtypeStruct((width, heads * TILE), f32)
    part, log_own, corr_own, gk_own, gv_own, gq_last, same = call(
        functools.partial(own_forward, heads, factor),
        [], arrays,
        [wide, line, line, grads, grads, tile_grads, jax.ShapeDtypeStruct((tiles,), jnp.int32)],
        [acc, single, single, columns, square], 6, "own_forward", scalar_outs=1,
    )
    past_part, log_total, corr, back, gq_part, size = call(
        functools.partial(crossing_kernel, heads, factor, scaling),
        [], [*arrays, past_a, past_b, part, log_own, corr_own],
        [wide, line, line, jax.ShapeDtypeStruct((4 * HALF, width), bf16), wide,
         jax.ShapeDtypeStruct((1,), jnp.int32)],
        [acc, single, single, square, square, gsum, gsum], 6, "crossing", scalar_outs=1,
    )
    came = send_back(back, along)
    full = jax.ShapeDtypeStruct((rows, heads * width), bf16)
    stage = pltpu.VMEM((HALF, heads * width), bf16)
    att, gq, att_b, gq_b, gkv_a, gkv_b = call(
        functools.partial(own_backward, heads, factor, scaling),
        [size, same],
        [*arrays, part, past_part, log_total, corr, gq_part, gk_own, gv_own, gq_last],
        [full, full, half_rows, half_rows, half_grad, half_grad],
        [acc, gsum, gsum, columns, stage, stage, pltpu.SemaphoreType.DMA((2,))], 6, "own_backward",
        specs=([VMEM] * 16, [ANY, ANY] + [VMEM] * 4),
    )
    att_b, gq_b = lax.optimization_barrier((att_b, gq_b))
    att_c, gq_c = send(att_b, swap), send(gq_b, swap)
    mine, give = call(
        add_kernel, [], [gkv_a, gkv_b, came], [half_back, half_back], [], 1, "add"
    )
    thin = jax.ShapeDtypeStruct((rows, width), bf16)
    attended, grad_queries, grad_keys, grad_values = call(
        place_kernel, [], [att, gq, att_c, gq_c, mine, send(give, swap)], [full, full, thin, thin],
        [pltpu.SemaphoreType.DMA((6,))], 1, "place",
        specs=([ANY] * 6, [ANY] * 4), aliases={0: 0, 1: 1},
    )
    return attended, grad_queries, grad_keys, grad_values


def solution(mesh):
    rows = P(AXES, None)
    return jax.shard_map(
        per_device,
        mesh=mesh,
        in_specs=(rows, rows, rows, rows, P(AXES)),
        out_specs=(rows, rows, rows, rows),
        check_vma=False,
    )
```

```python
import functools
import math

import jax
import jax.numpy as jnp
from jax import lax
from jax.experimental import pallas as pl
from jax.experimental.pallas import tpu as pltpu
from jax.sharding import PartitionSpec as P

AXES = ("outer", "inner")
TILE = 256
LANES = 128
HALF = 512
NOTES = 16
SLOTS = 6
HIDDEN = -1e30
NT = (((1,), (1,)), ((), ()))
TN = (((0,), (0,)), ((), ()))
NN = (((1,), (0,)), ((), ()))


def dot(a, b, dims):
    return lax.dot_general(a, b, dims, preferred_element_type=jnp.float32)


def core_of():
    return lax.rem(lax.axis_index("inner"), 2)


def stacked(pair, tile, heads):
    ref = pair[tile // 2]
    width = ref.shape[1] // heads
    rows = pl.ds(pl.multiple_of(core_of() * HALF + (tile % 2) * TILE, TILE), TILE)
    return jnp.concatenate(
        [ref[rows, h * width : (h + 1) * width] for h in range(heads)], axis=0
    )


def unstacked(columns, pair, tile, heads):
    ref = pair[tile // 2]
    width = ref.shape[1] // heads
    start = (tile % 2) * TILE
    rows = columns.astype(ref.dtype).T
    for h in range(heads):
        ref[start : start + TILE, h * width : (h + 1) * width] = rows[h * TILE : (h + 1) * TILE]


def keys_of(pair, key_tile):
    ref = pair[key_tile // 2]
    start = (key_tile % 2) * TILE
    if isinstance(ref, tuple):
        rows = pl.ds(pl.multiple_of(core_of() * HALF + start, TILE), TILE)
        return ref[0][rows, :], ref[1][rows, :]
    return ref[start : start + TILE, :], ref[HALF + start : HALF + start + TILE, :]


def segments_of(pair):
    rows = HALF // LANES
    parts = []
    for ref in pair:
        if isinstance(ref, tuple):
            own = ref[2][pl.ds(core_of() * rows, rows), :]
            parts.append(own.astype(jnp.float32))
            continue
        notes = ref[2 * HALF :, :].astype(jnp.float32)
        high, middle, low = (notes[i * rows : (i + 1) * rows] for i in range(3))
        parts.append(high * 4096.0 + middle * 64.0 + low)
    return jnp.concatenate(parts, axis=0)


def spread(segs, columns):
    for r in range(segs.shape[0]):
        block = jnp.broadcast_to(segs[r : r + 1, :], (LANES, LANES))
        columns[r * LANES : (r + 1) * LANES, :] = block.T


def own_bias(segs, columns, tile, key_tile, heads):
    per = TILE // LANES
    keys = columns[key_tile * TILE : (key_tile + 1) * TILE, :]
    parts = []
    for r in range(per):
        seen = keys == segs[tile * per + r : tile * per + r + 1, :]
        if tile == key_tile:
            key = lax.broadcasted_iota(jnp.int32, (TILE, LANES), 0)
            query = lax.broadcasted_iota(jnp.int32, (TILE, LANES), 1) + r * LANES
            seen = seen & (key <= query)
        parts.append(jnp.where(seen, 0.0, HIDDEN))
    return jnp.concatenate(parts * heads, axis=1)


def crossing_bias(first_key, crossing, tile, key_tile, heads):
    key = lax.broadcasted_iota(jnp.int32, (TILE, LANES), 0) + key_tile * TILE
    query = lax.broadcasted_iota(jnp.int32, (TILE, TILE), 1) + tile * TILE
    key = jnp.concatenate([key] * (TILE // LANES), axis=1)
    seen = jnp.where((key >= first_key) & (query < crossing), 0.0, HIDDEN)
    return jnp.concatenate([seen] * heads, axis=1)


def softmax_step(scores, values, log_ref, total_ref, acc):
    largest = log_ref[...]
    larger = jnp.maximum(largest, jnp.max(scores, axis=0, keepdims=True))
    shrink = jnp.exp2(largest - larger)
    weights = jnp.exp2(scores - larger)
    log_ref[...] = larger
    total_ref[...] = total_ref[...] * shrink + jnp.sum(weights, axis=0, keepdims=True)
    acc[...] = acc[...] * shrink + dot(values, weights.astype(jnp.bfloat16), TN)


def finish(tile, g, largest, total_ref, acc, part_ref, log_ref, corr_ref):
    total = total_ref[...]
    att = acc[...] / total
    rounded = att.astype(jnp.bfloat16).astype(jnp.float32)
    corr_ref[tile] = jnp.sum(rounded * g.T.astype(jnp.float32), axis=0, keepdims=True)
    log_ref[tile] = largest + jnp.log2(total)
    part_ref[tile] = att


def gradient_step(scores, keys, grown, q, g, log_total, corr, key_tile, gk, gv, gq):
    block = slice(key_tile * TILE, (key_tile + 1) * TILE)
    weights = jnp.exp2(scores - log_total)
    grad = (weights * (grown - corr)).astype(jnp.bfloat16)
    gv[block, :] += dot(weights.astype(jnp.bfloat16), g, NN)
    gk[block, :] += dot(grad, q, NN)
    gq[...] += dot(keys, grad, TN)


def pack_kernel(k_ref, v_ref, segs_ref, first_ref, second_ref, segs, stage, sems, out_sems):
    core = core_of()
    rows = HALF // LANES
    ids = pltpu.make_async_copy(segs_ref, segs, sems.at[4])
    ids.start()
    halves = ((0, first_ref, core), (1, second_ref, 1 - core))
    arriving = []
    for i, ref, half in halves:
        start = pl.ds(pl.multiple_of(half * HALF, HALF), HALF)
        for j, source in enumerate((k_ref, v_ref)):
            place = pl.ds(j * HALF, HALF)
            copy = pltpu.make_async_copy(source.at[start, :], stage.at[i, place, :], sems.at[2 * i + j])
            copy.start()
            arriving.append((copy, i, ref, place))
    ids.wait()
    leaving = []

    def leave(i, ref, place):
        copy = pltpu.make_async_copy(stage.at[i, place, :], ref.at[place, :], out_sems.at[len(leaving)])
        copy.start()
        leaving.append(copy)

    for i, ref, half in halves:
        own = segs[pl.ds(half * rows, rows), :]
        codes = [own >> 12, (own >> 6) & 63, own & 63, own & 0]
        codes = jnp.concatenate([code.astype(jnp.float32) for code in codes], axis=0)
        stage[i, 2 * HALF :, :] = codes.astype(jnp.bfloat16)
        leave(i, ref, pl.ds(2 * HALF, NOTES))
    for copy, i, ref, place in arriving:
        copy.wait()
        leave(i, ref, place)
    for copy in leaving:
        copy.wait()


def own_forward(
    heads, factor,
    q_a, q_b, g_a, g_b, k_a, v_a, ids_a, kv_b,
    part_ref, log_ref, corr_ref, gk, gv, gq_ref, same_ref, acc, largest, total, columns, kept,
):
    kv_a = (k_a, v_a, ids_a)
    segs = segments_of((kv_a, kv_b))
    spread(segs, columns)
    tiles = 2 * HALF // TILE
    per = TILE // LANES
    head = jnp.sum((segs == segs[:1, :1]).astype(jnp.float32)).astype(jnp.int32)
    ahead = head <= (tiles - 1) * TILE
    same_ref[0] = ahead.astype(jnp.int32)
    gk[...] = jnp.zeros_like(gk)
    gv[...] = jnp.zeros_like(gv)
    for tile in range(1, tiles):
        first = segs[tile * per : tile * per + 1, :1]
        same_ref[tile] = jnp.sum((segs[: tile * per] == first).astype(jnp.float32)).astype(jnp.int32)
    for tile in range(tiles):
        q = stacked((q_a, q_b), tile, heads)

        def step(key_tile):
            keys, values = keys_of((kv_a, kv_b), key_tile)
            scores = dot(keys, q, NT) * factor + own_bias(segs, columns, tile, key_tile, heads)
            if tile == tiles - 1:
                kept[key_tile] = scores
            if key_tile == tile:
                top = jnp.max(scores, axis=0, keepdims=True)
                weights = jnp.exp2(scores - top)
                largest[...] = top
                total[...] = jnp.sum(weights, axis=0, keepdims=True)
                acc[...] = dot(values, weights.astype(jnp.bfloat16), TN)
            else:
                softmax_step(scores, values, largest, total, acc)

        step(tile)
        for key_tile in reversed(range(tile)):

            @pl.when(same_ref[tile] > (tile - 1 - key_tile) * TILE)
            def _():
                step(key_tile)

        g = stacked((g_a, g_b), tile, heads)
        finish(tile, g, largest[...], total, acc, part_ref, log_ref, corr_ref)

    @pl.when(ahead)
    def _():
        gq_ref[...] = jnp.zeros_like(gq_ref)

        def grads(key_tile):
            keys, values = keys_of((kv_a, kv_b), key_tile)
            gradient_step(
                kept[key_tile], keys, dot(values, g, NT), q, g, log_ref[tile], corr_ref[tile],
                key_tile, gk, gv, gq_ref,
            )

        grads(tile)
        for key_tile in reversed(range(tile)):

            @pl.when(same_ref[tile] > (tile - 1 - key_tile) * TILE)
            def _():
                grads(key_tile)


def slot(tile, key_tile, tiles, first_key):
    lowest = first_key // TILE
    return jnp.minimum(tile * (tiles - lowest) + key_tile - lowest, SLOTS - 1)


def crossing_kernel(
    heads, factor, scaling,
    q_a, q_b, g_a, g_b, k_a, v_a, ids_a, kv_b, past_a, past_b, log_in, corr_in,
    log_ref, corr_ref, back_ref, weight_ref, grad_ref, size_ref,
    largest, total, product, kept, grown, gk, gv,
):
    rows = 2 * HALF
    tiles = rows // TILE
    log_ref[...] = log_in[...]
    corr_ref[...] = corr_in[...]
    gk[...] = jnp.zeros_like(gk)
    gv[...] = jnp.zeros_like(gv)
    segs = segments_of(((k_a, v_a, ids_a), kv_b))
    past = segments_of((past_a, past_b))
    first = segs[:1, :1]
    started = (lax.axis_index("outer") > 0) | (lax.axis_index("inner") > 0)
    tail = jnp.sum((past == first).astype(jnp.float32)).astype(jnp.int32)
    tail = jnp.where(started, tail, 0)
    head = jnp.sum((segs == first).astype(jnp.float32)).astype(jnp.int32)
    crossing = jnp.where(tail > 0, head, 0)
    first_key = rows - tail
    size_ref[0] = crossing
    size_ref[1] = first_key

    for tile in range(tiles):

        @pl.when(tile * TILE < crossing)
        def _():
            q = stacked((q_a, q_b), tile, heads)
            g = stacked((g_a, g_b), tile, heads)
            largest[...] = log_in[tile]
            total[...] = jnp.ones_like(total)
            product[...] = corr_in[tile]
            for key_tile in range(tile, tiles):

                @pl.when((key_tile + 1) * TILE > first_key)
                def _():
                    keys, values = keys_of((past_a, past_b), key_tile)
                    bias = crossing_bias(first_key, crossing, tile, key_tile, heads)
                    scores = dot(keys, q, NT) * factor + bias
                    grow = dot(values, g, NT)
                    kept[key_tile] = scores
                    grown[key_tile] = grow
                    top = largest[...]
                    larger = jnp.maximum(top, jnp.max(scores, axis=0, keepdims=True))
                    shrink = jnp.exp2(top - larger)
                    weights = jnp.exp2(scores - larger)
                    largest[...] = larger
                    total[...] = total[...] * shrink + jnp.sum(weights, axis=0, keepdims=True)
                    product[...] = product[...] * shrink + jnp.sum(
                        weights * grow, axis=0, keepdims=True
                    )

            log_total = largest[...] + jnp.log2(total[...])
            corr = product[...] / total[...]
            log_ref[tile] = log_total
            corr_ref[tile] = corr
            for key_tile in range(tile, tiles):

                @pl.when((key_tile + 1) * TILE > first_key)
                def _():
                    block = slice(key_tile * TILE, (key_tile + 1) * TILE)
                    weights = jnp.exp2(kept[key_tile] - log_total)
                    grad = (weights * (grown[key_tile] - corr)).astype(jnp.bfloat16)
                    weights = weights.astype(jnp.bfloat16)
                    gv[block, :] += dot(weights, g, NN)
                    gk[block, :] += dot(grad, q, NN)
                    place = slot(tile, key_tile, tiles, first_key)
                    weight_ref[place] = weights
                    grad_ref[place] = grad

    for start in (0, HALF):
        place = 2 * start
        block = slice(start, start + HALF)
        back_ref[place : place + HALF, :] = (gk[block, :] * scaling).astype(back_ref.dtype)
        back_ref[place + HALF : place + 2 * HALF, :] = gv[block, :].astype(back_ref.dtype)


def own_backward(
    heads, factor, scaling,
    size_ref, same_ref, q_a, q_b, g_a, g_b, k_a, v_a, ids_a, kv_b, past_a, past_b, part_ref, log_in, log_ref, corr_ref,
    weight_ref, grad_ref, gk_in, gv_in, gq_last,
    att_ref, gq_ref, att_b, gq_b, gkv_a, gkv_b, acc, gk, gv, columns, att_a, gq_a, sems,
):
    kv_a = (k_a, v_a, ids_a)
    segs = segments_of((kv_a, kv_b))
    spread(segs, columns)
    tiles = 2 * HALF // TILE
    gk[...] = gk_in[...]
    gv[...] = gv_in[...]
    mine = pl.ds(pl.multiple_of(core_of() * HALF, HALF), HALF)
    copies = [
        pltpu.make_async_copy(att_a, att_ref.at[mine, :], sems.at[0]),
        pltpu.make_async_copy(gq_a, gq_ref.at[mine, :], sems.at[1]),
    ]
    for tile in range(tiles):

        @pl.when(tile * TILE < size_ref[0])
        def _():
            acc[...] = part_ref[tile] * jnp.exp2(log_in[tile] - log_ref[tile])

            def add_past(which, ref):
                for key_tile in range(tile, tiles):

                    @pl.when((key_tile + 1) * TILE > size_ref[1])
                    def _():
                        rows = keys_of((past_a, past_b), key_tile)[which]
                        acc[...] += dot(rows, ref[slot(tile, key_tile, tiles, size_ref[1])], TN)

            add_past(1, weight_ref)
            unstacked(acc[...], (att_a, att_b), tile, heads)
            acc[...] = jnp.zeros_like(acc)
            add_past(0, grad_ref)

        @pl.when(tile * TILE >= size_ref[0])
        def _():
            acc[...] = jnp.zeros_like(acc)
            unstacked(part_ref[tile], (att_a, att_b), tile, heads)

        def steps():
            q = stacked((q_a, q_b), tile, heads)
            g = stacked((g_a, g_b), tile, heads)

            def step(key_tile):
                keys, values = keys_of((kv_a, kv_b), key_tile)
                scores = dot(keys, q, NT) * factor + own_bias(segs, columns, tile, key_tile, heads)
                gradient_step(
                    scores, keys, dot(values, g, NT), q, g, log_ref[tile], corr_ref[tile],
                    key_tile, gk, gv, acc,
                )

            step(tile)
            for key_tile in reversed(range(tile)):

                @pl.when(same_ref[tile] > (tile - 1 - key_tile) * TILE)
                def _():
                    step(key_tile)

        if tile < tiles - 1:
            steps()
        else:

            @pl.when(same_ref[0] == 0)
            def _():
                steps()

            @pl.when(same_ref[0] != 0)
            def _():
                acc[...] = gq_last[...]

        unstacked(acc[...] * scaling, (gq_a, gq_b), tile, heads)
        if tile == tiles // 2 - 1:
            for copy in copies:
                copy.start()
    for ref, start in ((gkv_a, 0), (gkv_b, HALF)):
        rows = slice(start, start + HALF)
        ref[:HALF, :] = gk[rows, :] * scaling
        ref[HALF:, :] = gv[rows, :]
    for copy in copies:
        copy.wait()


def add_kernel(gkv_a, gkv_b, came_ref, mine_ref, give_ref):
    for start, own, out in ((0, gkv_a, mine_ref), (2 * HALF, gkv_b, give_ref)):
        came = came_ref[start : start + 2 * HALF, :].astype(jnp.float32)
        out[...] = (own[...] + came).astype(out.dtype)


def place_kernel(att_in, gq_in, att_c, gq_c, mine_ref, other_ref, att_ref, gq_ref, gk_ref, gv_ref, sems):
    core = core_of()
    mine = pl.ds(pl.multiple_of(core * HALF, HALF), HALF)
    other = pl.ds(pl.multiple_of((1 - core) * HALF, HALF), HALF)
    key_rows = pl.ds(0, HALF)
    value_rows = pl.ds(HALF, HALF)
    moves = (
        (att_c, att_ref.at[other, :]),
        (gq_c, gq_ref.at[other, :]),
        (mine_ref.at[key_rows, :], gk_ref.at[mine, :]),
        (mine_ref.at[value_rows, :], gv_ref.at[mine, :]),
        (other_ref.at[key_rows, :], gk_ref.at[other, :]),
        (other_ref.at[value_rows, :], gv_ref.at[other, :]),
    )
    copies = [pltpu.make_async_copy(a, b, sems.at[i]) for i, (a, b) in enumerate(moves)]
    for copy in copies:
        copy.start()
    for copy in copies:
        copy.wait()


SMEM = pl.BlockSpec(memory_space=pltpu.SMEM)
VMEM = pl.BlockSpec(memory_space=pltpu.VMEM)
ANY = pl.BlockSpec(memory_space=pl.ANY)
HBM = pl.BlockSpec(memory_space=pltpu.HBM)


def call(kernel, scalars, arrays, outs, scratch, micros, name, scalar_outs=0, specs=None, room=30, aliases=None):
    arrived, left = specs or ([VMEM] * len(arrays), [VMEM] * (len(outs) - scalar_outs))
    return pl.pallas_call(
        kernel,
        out_shape=outs,
        in_specs=[SMEM] * len(scalars) + arrived,
        out_specs=left + [SMEM] * scalar_outs,
        scratch_shapes=scratch,
        compiler_params=pltpu.CompilerParams(vmem_limit_bytes=room * 2**20),
        cost_estimate=pl.CostEstimate(
            flops=int(micros * 1e9), bytes_accessed=2**20, transcendentals=0
        ),
        input_output_aliases=aliases or {},
        name=name,
    )(*scalars, *arrays)


def per_device(queries, key_rows, value_rows, grad_out, segments):
    count = lax.axis_size(AXES)
    rows, width = key_rows.shape
    heads = queries.shape[1] // width
    tiles = rows // TILE
    scaling = width ** (-0.5)
    factor = scaling * math.log2(math.e)
    swap = [(i, i ^ 1) for i in range(count)]
    along = (
        [(i, i + 2) for i in range(0, count - 2, 2)]
        + [(count - 2, count - 1)]
        + [(i + 2, i) for i in range(1, count - 2, 2)]
    )
    near = [(i, i + 1) for i in range(1, count - 2, 2)]
    near = near + [(b, a) for a, b in near] + [(count - 1, count - 1)]

    def send(array, pairs):
        return lax.ppermute(array, AXES, pairs)

    def send_back(array, pairs):
        return lax.ppermute(array, AXES, [(b, a) for a, b in pairs])

    f32 = jnp.float32
    bf16 = jnp.bfloat16
    segs = segments.reshape(rows // LANES, LANES)
    bundle = jax.ShapeDtypeStruct((2 * HALF + NOTES, width), bf16)
    first, second = call(
        pack_kernel, [], [key_rows, value_rows, segs], [bundle, bundle],
        [
            pltpu.VMEM(segs.shape, jnp.int32),
            pltpu.VMEM((2, 2 * HALF + NOTES, width), bf16),
            pltpu.SemaphoreType.DMA((5,)),
            pltpu.SemaphoreType.DMA((6,)),
        ], 1, "pack",
        specs=([HBM] * 3, [HBM] * 2), room=60,
    )
    first, second, queries, grad_out = lax.optimization_barrier(
        (first, second, queries, grad_out)
    )
    past_a = send(first, along)
    other = send(second, swap)
    other, second = lax.optimization_barrier((other, second))
    past_b = send(second, near)
    q_o, g_o = send(queries, swap), send(grad_out, swap)
    line = jax.ShapeDtypeStruct((tiles, 1, heads * TILE), f32)
    wide = jax.ShapeDtypeStruct((tiles, width, heads * TILE), f32)
    half_rows = jax.ShapeDtypeStruct((HALF, heads * width), bf16)
    half_back = jax.ShapeDtypeStruct((2 * HALF, width), bf16)
    half_grad = jax.ShapeDtypeStruct((2 * HALF, width), f32)
    acc = pltpu.VMEM((width, heads * TILE), f32)
    single = pltpu.VMEM((1, heads * TILE), f32)
    columns = pltpu.VMEM((rows, LANES), f32)
    gsum = pltpu.VMEM((rows, width), f32)
    square = pltpu.VMEM((tiles, TILE, heads * TILE), f32)
    arrays = [queries, q_o, grad_out, g_o, key_rows, value_rows, segs, other]
    grads = jax.ShapeDtypeStruct((rows, width), f32)
    tile_grads = jax.ShapeDtypeStruct((width, heads * TILE), f32)
    part, log_own, corr_own, gk_own, gv_own, gq_last, same = call(
        functools.partial(own_forward, heads, factor),
        [], arrays,
        [wide, line, line, grads, grads, tile_grads, jax.ShapeDtypeStruct((tiles,), jnp.int32)],
        [acc, single, single, columns, square], 6, "own_forward", scalar_outs=1,
    )
    slots = jax.ShapeDtypeStruct((SLOTS, TILE, heads * TILE), bf16)
    log_total, corr, back, weights, grad_scores, size = call(
        functools.partial(crossing_kernel, heads, factor, scaling),
        [], [*arrays, past_a, past_b, log_own, corr_own],
        [line, line, jax.ShapeDtypeStruct((4 * HALF, width), bf16), slots, slots,
         jax.ShapeDtypeStruct((2,), jnp.int32)],
        [single, single, single, square, square, gsum, gsum], 6, "crossing", scalar_outs=1,
    )
    came = send_back(back, along)
    full = jax.ShapeDtypeStruct((rows, heads * width), bf16)
    stage = pltpu.VMEM((HALF, heads * width), bf16)
    att, gq, att_b, gq_b, gkv_a, gkv_b = call(
        functools.partial(own_backward, heads, factor, scaling),
        [size, same],
        [*arrays, past_a, past_b, part, log_own, log_total, corr, weights, grad_scores, gk_own, gv_own,
         gq_last],
        [full, full, half_rows, half_rows, half_grad, half_grad],
        [acc, gsum, gsum, columns, stage, stage, pltpu.SemaphoreType.DMA((2,))], 6, "own_backward",
        specs=([VMEM] * 19, [ANY, ANY] + [VMEM] * 4),
    )
    att_b, gq_b = lax.optimization_barrier((att_b, gq_b))
    att_c, gq_c = send(att_b, swap), send(gq_b, swap)
    mine, give = call(
        add_kernel, [], [gkv_a, gkv_b, came], [half_back, half_back], [], 1, "add"
    )
    thin = jax.ShapeDtypeStruct((rows, width), bf16)
    attended, grad_queries, grad_keys, grad_values = call(
        place_kernel, [], [att, gq, att_c, gq_c, mine, send(give, swap)], [full, full, thin, thin],
        [pltpu.SemaphoreType.DMA((6,))], 1, "place",
        specs=([ANY] * 6, [ANY] * 4), aliases={0: 0, 1: 1},
    )
    return attended, grad_queries, grad_keys, grad_values


def solution(mesh):
    rows = P(AXES, None)
    return jax.shard_map(
        per_device,
        mesh=mesh,
        in_specs=(rows, rows, rows, rows, P(AXES)),
        out_specs=(rows, rows, rows, rows),
        check_vma=False,
    )
```

```python
import functools
import math

import jax
import jax.numpy as jnp
from jax import lax
from jax.experimental import pallas as pl
from jax.experimental.pallas import tpu as pltpu
from jax.sharding import PartitionSpec as P

AXES = ("outer", "inner")
TILE = 256
LANES = 128
HALF = 512
NOTES = 16
SLOTS = 6
HIDDEN = -1e30
NT = (((1,), (1,)), ((), ()))
TN = (((0,), (0,)), ((), ()))
NN = (((1,), (0,)), ((), ()))


def dot(a, b, dims):
    return lax.dot_general(a, b, dims, preferred_element_type=jnp.float32)


def core_of():
    return lax.rem(lax.axis_index("inner"), 2)


def stacked(pair, tile, heads):
    ref = pair[tile // 2]
    width = ref.shape[1] // heads
    rows = pl.ds(pl.multiple_of(core_of() * HALF + (tile % 2) * TILE, TILE), TILE)
    return jnp.concatenate(
        [ref[rows, h * width : (h + 1) * width] for h in range(heads)], axis=0
    )


def unstacked(columns, pair, tile, heads):
    ref = pair[tile // 2]
    width = ref.shape[1] // heads
    start = (tile % 2) * TILE
    rows = columns.astype(ref.dtype).T
    for h in range(heads):
        ref[start : start + TILE, h * width : (h + 1) * width] = rows[h * TILE : (h + 1) * TILE]


def keys_of(pair, key_tile):
    ref = pair[key_tile // 2]
    start = (key_tile % 2) * TILE
    if isinstance(ref, tuple):
        rows = pl.ds(pl.multiple_of(core_of() * HALF + start, TILE), TILE)
        return ref[0][rows, :], ref[1][rows, :]
    return ref[start : start + TILE, :], ref[HALF + start : HALF + start + TILE, :]


def segments_of(pair):
    rows = HALF // LANES
    parts = []
    for ref in pair:
        if isinstance(ref, tuple):
            own = ref[2][pl.ds(core_of() * rows, rows), :]
            parts.append(own.astype(jnp.float32))
            continue
        notes = ref[2 * HALF :, :].astype(jnp.float32)
        high, middle, low = (notes[i * rows : (i + 1) * rows] for i in range(3))
        parts.append(high * 4096.0 + middle * 64.0 + low)
    return jnp.concatenate(parts, axis=0)


def spread(segs, columns):
    for r in range(segs.shape[0]):
        block = jnp.broadcast_to(segs[r : r + 1, :], (LANES, LANES))
        columns[r * LANES : (r + 1) * LANES, :] = block.T


def own_bias(segs, columns, tile, key_tile, heads):
    per = TILE // LANES
    keys = columns[key_tile * TILE : (key_tile + 1) * TILE, :]
    parts = []
    for r in range(per):
        seen = keys == segs[tile * per + r : tile * per + r + 1, :]
        if tile == key_tile:
            key = lax.broadcasted_iota(jnp.int32, (TILE, LANES), 0)
            query = lax.broadcasted_iota(jnp.int32, (TILE, LANES), 1) + r * LANES
            seen = seen & (key <= query)
        parts.append(jnp.where(seen, 0.0, HIDDEN))
    return jnp.concatenate(parts * heads, axis=1)


def crossing_bias(first_key, crossing, tile, key_tile, heads):
    key = lax.broadcasted_iota(jnp.int32, (TILE, LANES), 0) + key_tile * TILE
    query = lax.broadcasted_iota(jnp.int32, (TILE, TILE), 1) + tile * TILE
    key = jnp.concatenate([key] * (TILE // LANES), axis=1)
    seen = jnp.where((key >= first_key) & (query < crossing), 0.0, HIDDEN)
    return jnp.concatenate([seen] * heads, axis=1)


def softmax_step(scores, values, log_ref, total_ref, acc):
    largest = log_ref[...]
    larger = jnp.maximum(largest, jnp.max(scores, axis=0, keepdims=True))
    shrink = jnp.exp2(largest - larger)
    weights = jnp.exp2(scores - larger)
    log_ref[...] = larger
    total_ref[...] = total_ref[...] * shrink + jnp.sum(weights, axis=0, keepdims=True)
    acc[...] = acc[...] * shrink + dot(values, weights.astype(jnp.bfloat16), TN)


def finish(tile, g, largest, total_ref, acc, part_ref, log_ref, corr_ref):
    total = total_ref[...]
    att = acc[...] / total
    rounded = att.astype(jnp.bfloat16).astype(jnp.float32)
    corr_ref[tile] = jnp.sum(rounded * g.T.astype(jnp.float32), axis=0, keepdims=True)
    log_ref[tile] = largest + jnp.log2(total)
    part_ref[tile] = att


def gradient_step(scores, keys, grown, q, g, log_total, corr, key_tile, gk, gv, gq):
    block = slice(key_tile * TILE, (key_tile + 1) * TILE)
    weights = jnp.exp2(scores - log_total)
    grad = (weights * (grown - corr)).astype(jnp.bfloat16)
    gv[block, :] += dot(weights.astype(jnp.bfloat16), g, NN)
    gk[block, :] += dot(grad, q, NN)
    gq[...] += dot(keys, grad, TN)


def diagonal_step(bias, keys, values, q, g, factor, log_total, corr, tile, gk, gv, gq, heads):
    half = TILE // 2

    def late(rows):
        return jnp.concatenate([rows[h * TILE + half : (h + 1) * TILE] for h in range(heads)], axis=0)

    def late_lanes(line):
        return jnp.concatenate(
            [line[:, h * TILE + half : (h + 1) * TILE] for h in range(heads)], axis=1
        )

    parts = (
        (0, q, g, log_total, corr, bias[:half]),
        (half, late(q), late(g), late_lanes(log_total), late_lanes(corr), late_lanes(bias[half:])),
    )
    for start, q_part, g_part, log_part, corr_part, bias_part in parts:
        block = slice(tile * TILE + start, tile * TILE + start + half)
        k_part = keys[start : start + half]
        scores = dot(k_part, q_part, NT) * factor + bias_part
        weights = jnp.exp2(scores - log_part)
        grown = dot(values[start : start + half], g_part, NT)
        grad = (weights * (grown - corr_part)).astype(jnp.bfloat16)
        gv[block, :] += dot(weights.astype(jnp.bfloat16), g_part, NN)
        gk[block, :] += dot(grad, q_part, NN)
        moved = dot(k_part, grad, TN)
        if start == 0:
            gq[...] += moved
        else:
            for h in range(heads):
                gq[:, h * TILE + half : (h + 1) * TILE] += moved[:, h * half : (h + 1) * half]


def pack_kernel(k_ref, v_ref, segs_ref, first_ref, second_ref, segs, stage, sems, out_sems):
    core = core_of()
    rows = HALF // LANES
    ids = pltpu.make_async_copy(segs_ref, segs, sems.at[4])
    ids.start()
    halves = ((0, first_ref, core), (1, second_ref, 1 - core))
    arriving = []
    for i, ref, half in halves:
        start = pl.ds(pl.multiple_of(half * HALF, HALF), HALF)
        for j, source in enumerate((k_ref, v_ref)):
            place = pl.ds(j * HALF, HALF)
            copy = pltpu.make_async_copy(source.at[start, :], stage.at[i, place, :], sems.at[2 * i + j])
            copy.start()
            arriving.append((copy, i, ref, place))
    ids.wait()
    leaving = []

    def leave(i, ref, place):
        copy = pltpu.make_async_copy(stage.at[i, place, :], ref.at[place, :], out_sems.at[len(leaving)])
        copy.start()
        leaving.append(copy)

    for i, ref, half in halves:
        own = segs[pl.ds(half * rows, rows), :]
        codes = [own >> 12, (own >> 6) & 63, own & 63, own & 0]
        codes = jnp.concatenate([code.astype(jnp.float32) for code in codes], axis=0)
        stage[i, 2 * HALF :, :] = codes.astype(jnp.bfloat16)
        leave(i, ref, pl.ds(2 * HALF, NOTES))
    for copy, i, ref, place in arriving:
        copy.wait()
        leave(i, ref, place)
    for copy in leaving:
        copy.wait()


def own_forward(
    heads, factor,
    q_a, q_b, g_a, g_b, k_a, v_a, ids_a, kv_b,
    part_ref, log_ref, corr_ref, gk, gv, gq_ref, same_ref, acc, largest, total, columns, kept,
):
    kv_a = (k_a, v_a, ids_a)
    segs = segments_of((kv_a, kv_b))
    spread(segs, columns)
    tiles = 2 * HALF // TILE
    per = TILE // LANES
    head = jnp.sum((segs == segs[:1, :1]).astype(jnp.float32)).astype(jnp.int32)
    ahead = head <= (tiles - 1) * TILE
    same_ref[0] = ahead.astype(jnp.int32)
    gk[...] = jnp.zeros_like(gk)
    gv[...] = jnp.zeros_like(gv)
    for tile in range(1, tiles):
        first = segs[tile * per : tile * per + 1, :1]
        same_ref[tile] = jnp.sum((segs[: tile * per] == first).astype(jnp.float32)).astype(jnp.int32)
    for tile in range(tiles):
        q = stacked((q_a, q_b), tile, heads)

        def step(key_tile):
            keys, values = keys_of((kv_a, kv_b), key_tile)
            scores = dot(keys, q, NT) * factor + own_bias(segs, columns, tile, key_tile, heads)
            if tile == tiles - 1:
                kept[key_tile] = scores
            if key_tile == tile:
                top = jnp.max(scores, axis=0, keepdims=True)
                weights = jnp.exp2(scores - top)
                largest[...] = top
                total[...] = jnp.sum(weights, axis=0, keepdims=True)
                acc[...] = dot(values, weights.astype(jnp.bfloat16), TN)
            else:
                softmax_step(scores, values, largest, total, acc)

        step(tile)
        for key_tile in reversed(range(tile)):

            @pl.when(same_ref[tile] > (tile - 1 - key_tile) * TILE)
            def _():
                step(key_tile)

        g = stacked((g_a, g_b), tile, heads)
        finish(tile, g, largest[...], total, acc, part_ref, log_ref, corr_ref)

    @pl.when(ahead)
    def _():
        gq_ref[...] = jnp.zeros_like(gq_ref)

        def grads(key_tile):
            keys, values = keys_of((kv_a, kv_b), key_tile)
            gradient_step(
                kept[key_tile], keys, dot(values, g, NT), q, g, log_ref[tile], corr_ref[tile],
                key_tile, gk, gv, gq_ref,
            )

        grads(tile)
        for key_tile in reversed(range(tile)):

            @pl.when(same_ref[tile] > (tile - 1 - key_tile) * TILE)
            def _():
                grads(key_tile)


def slot(tile, key_tile, tiles, first_key):
    lowest = first_key // TILE
    return jnp.minimum(tile * (tiles - lowest) + key_tile - lowest, SLOTS - 1)


def crossing_kernel(
    heads, factor, scaling,
    q_a, q_b, g_a, g_b, k_a, v_a, ids_a, kv_b, past_a, past_b, log_in, corr_in,
    log_ref, corr_ref, back_ref, weight_ref, grad_ref, size_ref,
    largest, total, product, kept, grown, gk, gv,
):
    rows = 2 * HALF
    tiles = rows // TILE
    log_ref[...] = log_in[...]
    corr_ref[...] = corr_in[...]
    gk[...] = jnp.zeros_like(gk)
    gv[...] = jnp.zeros_like(gv)
    segs = segments_of(((k_a, v_a, ids_a), kv_b))
    past = segments_of((past_a, past_b))
    first = segs[:1, :1]
    started = (lax.axis_index("outer") > 0) | (lax.axis_index("inner") > 0)
    tail = jnp.sum((past == first).astype(jnp.float32)).astype(jnp.int32)
    tail = jnp.where(started, tail, 0)
    head = jnp.sum((segs == first).astype(jnp.float32)).astype(jnp.int32)
    crossing = jnp.where(tail > 0, head, 0)
    first_key = rows - tail
    size_ref[0] = crossing
    size_ref[1] = first_key

    for tile in range(tiles):

        @pl.when(tile * TILE < crossing)
        def _():
            q = stacked((q_a, q_b), tile, heads)
            g = stacked((g_a, g_b), tile, heads)
            largest[...] = log_in[tile]
            total[...] = jnp.ones_like(total)
            product[...] = corr_in[tile]
            for key_tile in range(tile, tiles):

                @pl.when((key_tile + 1) * TILE > first_key)
                def _():
                    keys, values = keys_of((past_a, past_b), key_tile)
                    bias = crossing_bias(first_key, crossing, tile, key_tile, heads)
                    scores = dot(keys, q, NT) * factor + bias
                    grow = dot(values, g, NT)
                    kept[key_tile] = scores
                    grown[key_tile] = grow
                    top = largest[...]
                    larger = jnp.maximum(top, jnp.max(scores, axis=0, keepdims=True))
                    shrink = jnp.exp2(top - larger)
                    weights = jnp.exp2(scores - larger)
                    largest[...] = larger
                    total[...] = total[...] * shrink + jnp.sum(weights, axis=0, keepdims=True)
                    product[...] = product[...] * shrink + jnp.sum(
                        weights * grow, axis=0, keepdims=True
                    )

            log_total = largest[...] + jnp.log2(total[...])
            corr = product[...] / total[...]
            log_ref[tile] = log_total
            corr_ref[tile] = corr
            for key_tile in range(tile, tiles):

                @pl.when((key_tile + 1) * TILE > first_key)
                def _():
                    block = slice(key_tile * TILE, (key_tile + 1) * TILE)
                    weights = jnp.exp2(kept[key_tile] - log_total)
                    grad = (weights * (grown[key_tile] - corr)).astype(jnp.bfloat16)
                    weights = weights.astype(jnp.bfloat16)
                    gv[block, :] += dot(weights, g, NN)
                    gk[block, :] += dot(grad, q, NN)
                    place = slot(tile, key_tile, tiles, first_key)
                    weight_ref[place] = weights
                    grad_ref[place] = grad

    for start in (0, HALF):
        place = 2 * start
        block = slice(start, start + HALF)
        back_ref[place : place + HALF, :] = (gk[block, :] * scaling).astype(back_ref.dtype)
        back_ref[place + HALF : place + 2 * HALF, :] = gv[block, :].astype(back_ref.dtype)


def own_backward(
    heads, factor, scaling,
    size_ref, same_ref, q_a, q_b, g_a, g_b, k_a, v_a, ids_a, kv_b, past_a, past_b, part_ref, log_in, log_ref, corr_ref,
    weight_ref, grad_ref, gk_in, gv_in, gq_last,
    att_ref, gq_ref, give_ref, gkv_a, gkv_b, acc, gk, gv, columns, att_a, gq_a, sems,
):
    kv_a = (k_a, v_a, ids_a)
    att_b, gq_b = give_ref.at[:HALF], give_ref.at[HALF:]
    segs = segments_of((kv_a, kv_b))
    spread(segs, columns)
    tiles = 2 * HALF // TILE
    gk[...] = gk_in[...]
    gv[...] = gv_in[...]
    mine = pl.ds(pl.multiple_of(core_of() * HALF, HALF), HALF)
    copies = [
        pltpu.make_async_copy(att_a, att_ref.at[mine, :], sems.at[0]),
        pltpu.make_async_copy(gq_a, gq_ref.at[mine, :], sems.at[1]),
    ]
    for tile in range(tiles):

        @pl.when(tile * TILE < size_ref[0])
        def _():
            acc[...] = part_ref[tile] * jnp.exp2(log_in[tile] - log_ref[tile])

            def add_past(which, ref):
                for key_tile in range(tile, tiles):

                    @pl.when((key_tile + 1) * TILE > size_ref[1])
                    def _():
                        rows = keys_of((past_a, past_b), key_tile)[which]
                        acc[...] += dot(rows, ref[slot(tile, key_tile, tiles, size_ref[1])], TN)

            add_past(1, weight_ref)
            unstacked(acc[...], (att_a, att_b), tile, heads)
            acc[...] = jnp.zeros_like(acc)
            add_past(0, grad_ref)

        @pl.when(tile * TILE >= size_ref[0])
        def _():
            acc[...] = jnp.zeros_like(acc)
            unstacked(part_ref[tile], (att_a, att_b), tile, heads)

        def steps():
            q = stacked((q_a, q_b), tile, heads)
            g = stacked((g_a, g_b), tile, heads)

            def step(key_tile):
                keys, values = keys_of((kv_a, kv_b), key_tile)
                scores = dot(keys, q, NT) * factor + own_bias(segs, columns, tile, key_tile, heads)
                gradient_step(
                    scores, keys, dot(values, g, NT), q, g, log_ref[tile], corr_ref[tile],
                    key_tile, gk, gv, acc,
                )

            keys, values = keys_of((kv_a, kv_b), tile)
            diagonal_step(
                own_bias(segs, columns, tile, tile, heads), keys, values, q, g, factor, log_ref[tile],
                corr_ref[tile], tile, gk, gv, acc, heads,
            )
            for key_tile in reversed(range(tile)):

                @pl.when(same_ref[tile] > (tile - 1 - key_tile) * TILE)
                def _():
                    step(key_tile)

        if tile < tiles - 1:
            steps()
        else:

            @pl.when(same_ref[0] == 0)
            def _():
                steps()

            @pl.when(same_ref[0] != 0)
            def _():
                acc[...] = gq_last[...]

        unstacked(acc[...] * scaling, (gq_a, gq_b), tile, heads)
        if tile == tiles // 2 - 1:
            for copy in copies:
                copy.start()
    for ref, start in ((gkv_a, 0), (gkv_b, HALF)):
        rows = slice(start, start + HALF)
        ref[:HALF, :] = gk[rows, :] * scaling
        ref[HALF:, :] = gv[rows, :]
    for copy in copies:
        copy.wait()


def add_kernel(gkv_a, gkv_b, came_ref, mine_ref, give_ref):
    for start, own, out in ((0, gkv_a, mine_ref), (2 * HALF, gkv_b, give_ref)):
        came = came_ref[start : start + 2 * HALF, :].astype(jnp.float32)
        out[...] = (own[...] + came).astype(out.dtype)


def place_kernel(att_in, gq_in, rows_ref, mine_ref, other_ref, att_ref, gq_ref, gk_ref, gv_ref, sems):
    core = core_of()
    mine = pl.ds(pl.multiple_of(core * HALF, HALF), HALF)
    other = pl.ds(pl.multiple_of((1 - core) * HALF, HALF), HALF)
    upper = pl.ds(0, HALF)
    lower = pl.ds(HALF, HALF)
    moves = (
        (rows_ref.at[upper, :], att_ref.at[other, :]),
        (rows_ref.at[lower, :], gq_ref.at[other, :]),
        (mine_ref.at[upper, :], gk_ref.at[mine, :]),
        (mine_ref.at[lower, :], gv_ref.at[mine, :]),
        (other_ref.at[upper, :], gk_ref.at[other, :]),
        (other_ref.at[lower, :], gv_ref.at[other, :]),
    )
    copies = [pltpu.make_async_copy(a, b, sems.at[i]) for i, (a, b) in enumerate(moves)]
    for copy in copies:
        copy.start()
    for copy in copies:
        copy.wait()


SMEM = pl.BlockSpec(memory_space=pltpu.SMEM)
VMEM = pl.BlockSpec(memory_space=pltpu.VMEM)
ANY = pl.BlockSpec(memory_space=pl.ANY)
HBM = pl.BlockSpec(memory_space=pltpu.HBM)


def call(kernel, scalars, arrays, outs, scratch, micros, name, scalar_outs=0, specs=None, room=30, aliases=None):
    arrived, left = specs or ([VMEM] * len(arrays), [VMEM] * (len(outs) - scalar_outs))
    return pl.pallas_call(
        kernel,
        out_shape=outs,
        in_specs=[SMEM] * len(scalars) + arrived,
        out_specs=left + [SMEM] * scalar_outs,
        scratch_shapes=scratch,
        compiler_params=pltpu.CompilerParams(vmem_limit_bytes=room * 2**20),
        cost_estimate=pl.CostEstimate(
            flops=int(micros * 1e9), bytes_accessed=2**20, transcendentals=0
        ),
        input_output_aliases=aliases or {},
        name=name,
    )(*scalars, *arrays)


def per_device(queries, key_rows, value_rows, grad_out, segments):
    count = lax.axis_size(AXES)
    rows, width = key_rows.shape
    heads = queries.shape[1] // width
    tiles = rows // TILE
    scaling = width ** (-0.5)
    factor = scaling * math.log2(math.e)
    swap = [(i, i ^ 1) for i in range(count)]
    along = (
        [(i, i + 2) for i in range(0, count - 2, 2)]
        + [(count - 2, count - 1)]
        + [(i + 2, i) for i in range(1, count - 2, 2)]
    )
    near = [(i, i + 1) for i in range(1, count - 2, 2)]
    near = near + [(b, a) for a, b in near] + [(count - 1, count - 1)]

    def send(array, pairs):
        return lax.ppermute(array, AXES, pairs)

    def send_back(array, pairs):
        return lax.ppermute(array, AXES, [(b, a) for a, b in pairs])

    f32 = jnp.float32
    bf16 = jnp.bfloat16
    segs = segments.reshape(rows // LANES, LANES)
    bundle = jax.ShapeDtypeStruct((2 * HALF + NOTES, width), bf16)
    first, second = call(
        pack_kernel, [], [key_rows, value_rows, segs], [bundle, bundle],
        [
            pltpu.VMEM(segs.shape, jnp.int32),
            pltpu.VMEM((2, 2 * HALF + NOTES, width), bf16),
            pltpu.SemaphoreType.DMA((5,)),
            pltpu.SemaphoreType.DMA((6,)),
        ], 1, "pack",
        specs=([HBM] * 3, [HBM] * 2), room=60,
    )
    first, second, queries, grad_out = lax.optimization_barrier(
        (first, second, queries, grad_out)
    )
    past_a = send(first, along)
    other = send(second, swap)
    other, second = lax.optimization_barrier((other, second))
    past_b = send(second, near)
    q_o, g_o = send(queries, swap), send(grad_out, swap)
    line = jax.ShapeDtypeStruct((tiles, 1, heads * TILE), f32)
    wide = jax.ShapeDtypeStruct((tiles, width, heads * TILE), f32)
    half_back = jax.ShapeDtypeStruct((2 * HALF, width), bf16)
    half_grad = jax.ShapeDtypeStruct((2 * HALF, width), f32)
    acc = pltpu.VMEM((width, heads * TILE), f32)
    single = pltpu.VMEM((1, heads * TILE), f32)
    columns = pltpu.VMEM((rows, LANES), f32)
    gsum = pltpu.VMEM((rows, width), f32)
    square = pltpu.VMEM((tiles, TILE, heads * TILE), f32)
    arrays = [queries, q_o, grad_out, g_o, key_rows, value_rows, segs, other]
    grads = jax.ShapeDtypeStruct((rows, width), f32)
    tile_grads = jax.ShapeDtypeStruct((width, heads * TILE), f32)
    part, log_own, corr_own, gk_own, gv_own, gq_last, same = call(
        functools.partial(own_forward, heads, factor),
        [], arrays,
        [wide, line, line, grads, grads, tile_grads, jax.ShapeDtypeStruct((tiles,), jnp.int32)],
        [acc, single, single, columns, square], 6, "own_forward", scalar_outs=1,
    )
    slots = jax.ShapeDtypeStruct((SLOTS, TILE, heads * TILE), bf16)
    log_total, corr, back, weights, grad_scores, size = call(
        functools.partial(crossing_kernel, heads, factor, scaling),
        [], [*arrays, past_a, past_b, log_own, corr_own],
        [line, line, jax.ShapeDtypeStruct((4 * HALF, width), bf16), slots, slots,
         jax.ShapeDtypeStruct((2,), jnp.int32)],
        [single, single, single, square, square, gsum, gsum], 6, "crossing", scalar_outs=1,
    )
    came = send_back(back, along)
    full = jax.ShapeDtypeStruct((rows, heads * width), bf16)
    stage = pltpu.VMEM((HALF, heads * width), bf16)
    att, gq, rows_b, gkv_a, gkv_b = call(
        functools.partial(own_backward, heads, factor, scaling),
        [size, same],
        [*arrays, past_a, past_b, part, log_own, log_total, corr, weights, grad_scores, gk_own, gv_own,
         gq_last],
        [full, full, full, half_grad, half_grad],
        [acc, gsum, gsum, columns, stage, stage, pltpu.SemaphoreType.DMA((2,))], 6, "own_backward",
        specs=([VMEM] * 19, [ANY, ANY] + [VMEM] * 3),
    )
    mine, give = call(
        add_kernel, [], [gkv_a, gkv_b, came], [half_back, half_back], [], 20, "add"
    )
    thin = jax.ShapeDtypeStruct((rows, width), bf16)
    attended, grad_queries, grad_keys, grad_values = call(
        place_kernel, [], [att, gq, send(rows_b, swap), mine, send(give, swap)], [full, full, thin, thin],
        [pltpu.SemaphoreType.DMA((6,))], 1, "place",
        specs=([ANY] * 5, [ANY] * 4), aliases={0: 0, 1: 1},
    )
    return attended, grad_queries, grad_keys, grad_values


def solution(mesh):
    rows = P(AXES, None)
    return jax.shard_map(
        per_device,
        mesh=mesh,
        in_specs=(rows, rows, rows, rows, P(AXES)),
        out_specs=(rows, rows, rows, rows),
        check_vma=False,
    )
```
